32 devices in a mesh: groups: 2 (over y), ctx: 16 (over z, x, core), dp: 1.
Axes of the slice: x: 2, y: 2, z: 4, core: 2. Of those that a mesh axis runs over, the one named last changes fastest.
Arguments:
- tokens: bfloat16 [4096, 1024], P(('groups', 'ctx', 'dp')), parts along dimension 0, may hold values from -6 to 6
- cotangent: bfloat16 [4096, 1024], P(('groups', 'ctx', 'dp')), parts along dimension 0, may hold values from -6 to 6
- expert_ids: int32 [4096, 8], P(('groups', 'ctx', 'dp')), parts along dimension 0, may hold values from 0 to 15, all different within a row; in each aligned block of 128 rows (0 to 127, 128 to 255, ...) at most 80 rows name the same one
- router_weights: float32 [4096, 8], P(('groups', 'ctx', 'dp')), parts along dimension 0, may hold values from 0.03 to 0.3
- seq_lengths: int32 [8], P('groups'), parts along dimension 0, may hold values from 256 to 768, as said below
- w_gate: bfloat16 [16, 1024, 384], P('ctx', 'dp'), may hold values from -0.1875 to 0.1875
- w_up: bfloat16 [16, 1024, 384], P('ctx', 'dp'), may hold values from -0.1875 to 0.1875
- w_down: bfloat16 [16, 384, 1024], P('ctx', None, 'dp'), may hold values from -0.3125 to 0.3125
Outputs:
- mixed: bfloat16 [4096, 1024], P(('groups', 'ctx', 'dp')), parts along dimension 0
- token_grads: bfloat16 [4096, 1024], P(('groups', 'ctx', 'dp')), parts along dimension 0
- weight_grads: float32 [4096, 8], P(('groups', 'ctx', 'dp')), parts along dimension 0
The draws below stay inside these ranges and needn't reach their ends.
There are 2 independent parts, one for each index of `groups`. The reference program is written for one: setup_inputs(seed, part) draws one part's arguments, and reference() takes and returns one part's arrays. A program takes and returns all parts, laid end to end along the dimension named above; an argument that names none is the same for every part. Nothing has to cross between parts.
Inputs may be any that keep to these rules, and one draw needn't show every extreme that they name: `expert_ids`: in each aligned block of 128 rows (the rows of one device) every expert is named by at most 80 rows, and in every draw some expert is named by exactly 80 rows of some block; the 8 entries of a row differ. `seq_lengths`: the 4 lengths sum to 2048; both ends of the range are reached in every draw.
All inputs are finite; a program needn't handle non-finite values.
Results may differ from the reference program's by a relative error of at most 0.0064.
Values may be sent and summed in bfloat16 or wider, within the bound.
A program may use at most 128 MiB of HBM per device.

```python
import math
import jax
import jax.numpy as jnp
import numpy as np
from jax import lax

D = 1024
FF = 384
TOPK = 8
TOK_DEV = 128
EXPERTS = 16
CAP = 80
TOKENS = 2048
NSEQ = 4
AVG_LEN = 512


def draw_seq_lengths(key, part):
    half_span = AVG_LEN // 2
    offsets = jax.random.randint(jax.random.fold_in(key, 11), (NSEQ // 2,), 0, half_span + 1)
    offsets = offsets.at[0].set(half_span)
    paired = jnp.stack([AVG_LEN + offsets, AVG_LEN - offsets], axis=1).reshape(NSEQ)
    order = jax.random.permutation(jax.random.fold_in(key, 23), NSEQ)
    return paired[order].astype(jnp.int32)


def shard_levels(own_key, shape, split, least, largest):
    def one(dim, blocks):
        draws = jax.random.uniform(jax.random.fold_in(jax.random.fold_in(own_key, 6), dim), (blocks,), jnp.float32, least / len(split), largest / len(split))
        return jnp.repeat(jnp.exp(draws), shape[dim] // blocks).reshape((-1,) + (1,) * (len(shape) - dim - 1))

    factor_of = one(*split[0])
    for cut in split[1:]:
        factor_of = factor_of * one(*cut)
    return factor_of


def shared_out(stream_key, own, number, rows, number_of, top, limit, skew):
    sequence = jax.random.permutation(stream_key, number_of)
    crowded, usual = portions_of(number_of, rows * top, limit, skew, True), portions_of(number_of, rows * top, limit, skew, False)
    places = jnp.arange(number_of)

    def named(lengths, rotation):
        used = int((lengths > 0).sum())
        fixed = max(1, used // 4)
        shifted = fixed + (places - fixed + rotation * (used - fixed)) % max(1, number_of - fixed)
        return jnp.zeros((number_of,), jnp.int32).at[sequence[jnp.where(places < fixed, places, shifted)]].set(jnp.asarray(lengths, jnp.int32))

    lengths = jnp.where(number % 4 == 0, named(crowded, number // 4), named(usual, number - number // 4 - 1))
    mixed = jax.random.permutation(jax.random.fold_in(own, 3), number_of)
    donor, taker = mixed[0:number_of // 2 * 2:2], mixed[1:number_of // 2 * 2:2]
    margin = jnp.minimum(lengths[donor] - 1, limit - lengths[taker]) // 2
    margin = jnp.where((donor == sequence[0]) | (taker == sequence[0]) | (lengths[taker] == 0), 0, jnp.maximum(margin, 0))
    shifted = jax.random.randint(jax.random.fold_in(own, 4), (number_of // 2,), 0, 1 << 20) % (margin + 1)
    lengths = lengths.at[donor].add(-shifted).at[taker].add(shifted)
    members = jnp.searchsorted(jnp.cumsum(lengths), jnp.arange(rows * top), side="right").astype(jnp.int32)
    table = members.reshape(top, rows).T
    table = table[jax.random.permutation(jax.random.fold_in(own, 1), rows)]
    rotation = jax.random.randint(jax.random.fold_in(own, 2), (rows, 1), 0, top)
    return jnp.take_along_axis(table, (jnp.arange(top)[None, :] + rotation) % top, axis=1)


def portions_of(number_of, total, limit, lean, full):
    weights = [(1 << 20) // math.isqrt(standing ** lean) + 1 for standing in range(1, number_of + 1)]
    largest = limit if full else min(limit, max(-(-total // number_of), total * weights[0] // sum(weights)))
    least = 1 if total - largest >= number_of - 1 else 0
    holding, rest = [largest] + [least] * (number_of - 1), total - largest - least * (number_of - 1)
    while rest > 0:
        movable = [i for i in range(1, number_of) if holding[i] < largest] or [i for i in range(1, number_of) if holding[i] < limit]
        whole, left = sum([weights[i] for i in movable]), rest
        for i in movable:
            addition = min(limit - holding[i], max(1, left * weights[i] // whole), rest)
            holding[i] = holding[i] + addition
            rest = rest - addition
    return np.array(holding)


def normal_values(rng, extent, scale, most, pieces=(), held_as=jnp.bfloat16):
    entries = jax.random.normal(rng, extent, jnp.float32) * scale
    if len(pieces) > 0:
        entries = shard_levels(rng, extent, pieces, -0.22, 0.18) * entries
    return jnp.clip(entries, min=-most, max=most).astype(held_as)


def setup_inputs(seed: int = 0, part: int = 0) -> dict:
    key_list = jax.random.split(jax.random.key(seed), 9)
    part_splits = jax.random.split(jax.random.fold_in(key_list[8], part), 9)
    tokens = normal_values(part_splits[0], (TOKENS, D), 1.0, 6.0, ((0, 16),))
    cotangent = normal_values(part_splits[1], (TOKENS, D), 1.0, 6.0, ((0, 16),))
    expert_ids_keys = jax.random.split(jax.random.fold_in(part_splits[2], 1), TOKENS // TOK_DEV)
    expert_ids_turns = jax.random.permutation(jax.random.fold_in(part_splits[2], 3), TOKENS // TOK_DEV)
    expert_ids = jax.vmap(lambda own, number: shared_out(jax.random.fold_in(part_splits[2], 2), own, number, TOK_DEV, EXPERTS, TOPK, CAP, 2))(expert_ids_keys, expert_ids_turns).reshape((TOKENS, TOPK))
    router_weights = jnp.clip(jnp.exp(math.log(0.3) - 2.3025852 * jax.random.uniform(part_splits[3], (TOKENS, TOPK), jnp.float32) ** shard_levels(part_splits[3], (TOKENS, TOPK), ((0, 16),), -0.2, 0.2)), 0.03, 0.3)
    seq_lengths = draw_seq_lengths(jax.random.fold_in(jax.random.fold_in(key_list[8], part), 71), part)
    w_gate = normal_values(key_list[5], (EXPERTS, D, FF), D ** -0.5, 0.1875, ((0, 16),))
    w_up = normal_values(key_list[6], (EXPERTS, D, FF), D ** -0.5, 0.1875, ((0, 16),))
    w_down = normal_values(key_list[7], (EXPERTS, FF, D), FF ** -0.5, 0.3125, ((0, 16),))
    return {"tokens": tokens, "cotangent": cotangent, "expert_ids": expert_ids, "router_weights": router_weights, "seq_lengths": seq_lengths, "w_gate": w_gate, "w_up": w_up, "w_down": w_down}


def loss_scale(position, seq_lengths, mean_length):
    ends = jnp.cumsum(seq_lengths).astype(jnp.int32)
    starts = ends - seq_lengths
    inside = (position[:, None] >= starts[None, :]) & (position[:, None] < ends[None, :])
    own_length = jnp.sum(jnp.where(inside, seq_lengths[None, :], 0), axis=1)
    return mean_length / own_length.astype(jnp.float32)


def forward_rows(slot_rows, gate_full, up_full, down_full):
    gate_pre = jnp.dot(slot_rows, gate_full, preferred_element_type=jnp.float32)
    up_value = jnp.dot(slot_rows, up_full, preferred_element_type=jnp.float32)
    activated = jax.nn.silu(gate_pre)
    hidden = (activated * up_value).astype(jnp.bfloat16)
    expert_out = jnp.dot(hidden, down_full, preferred_element_type=jnp.float32).astype(jnp.bfloat16)
    return gate_pre, up_value, activated, expert_out


def backward_rows(grad_rows, gate_pre, up_value, activated, gate_full, up_full, down_full):
    contract = (((1,), (1,)), ((), ()))
    hidden_grad = lax.dot_general(grad_rows, down_full, contract, preferred_element_type=jnp.float32)
    sigmoid_value = jax.nn.sigmoid(gate_pre)
    silu_slope = sigmoid_value * (1.0 + gate_pre * (1.0 - sigmoid_value))
    gate_grad = (hidden_grad * up_value * silu_slope).astype(jnp.bfloat16)
    up_grad = (hidden_grad * activated).astype(jnp.bfloat16)
    slot_grad = lax.dot_general(gate_grad, gate_full, contract, preferred_element_type=jnp.float32)
    slot_grad = slot_grad + lax.dot_general(up_grad, up_full, contract, preferred_element_type=jnp.float32)
    return slot_grad.astype(jnp.bfloat16)


def reference(tokens, cotangent, expert_ids, router_weights, seq_lengths, w_gate, w_up, w_down):
    position = jnp.arange(TOKENS, dtype=jnp.int32)
    loss_weight = loss_scale(position, seq_lengths, AVG_LEN * 1.0)
    out_grad = (cotangent.astype(jnp.float32) * loss_weight[:, None]).astype(jnp.bfloat16)
    assign_total = TOKENS * TOPK
    flat_ids = expert_ids.reshape(-1)
    flat_weights = router_weights.reshape(-1)
    slot_total = (TOKENS // TOK_DEV) * CAP

    def per_expert(carry, expert_index):
        mixed_sum, grad_sum, weight_flat = carry
        picked = jnp.nonzero(flat_ids == expert_index, size=slot_total, fill_value=assign_total)[0].astype(jnp.int32)
        filled = picked < assign_total
        clipped = jnp.minimum(picked, assign_total - 1)
        token_of = clipped // TOPK
        slot_rows = jnp.where(filled[:, None], tokens[token_of], jnp.zeros((), jnp.bfloat16))
        grad_rows = jnp.where(filled[:, None], out_grad[token_of], jnp.zeros((), jnp.bfloat16))
        slot_weights = jnp.where(filled, flat_weights[clipped], 0.0)
        gate_full = w_gate[expert_index]
        up_full = w_up[expert_index]
        down_full = w_down[expert_index]
        gate_pre, up_value, activated, expert_out = forward_rows(slot_rows, gate_full, up_full, down_full)
        slot_grad = backward_rows(grad_rows, gate_pre, up_value, activated, gate_full, up_full, down_full)
        mixed_sum = mixed_sum.at[token_of].add(slot_weights[:, None] * expert_out.astype(jnp.float32))
        grad_sum = grad_sum.at[token_of].add(slot_weights[:, None] * slot_grad.astype(jnp.float32))
        inner = jnp.sum(grad_rows.astype(jnp.float32) * expert_out.astype(jnp.float32), axis=1)
        weight_flat = weight_flat.at[picked].set(inner, mode="drop")
        return (mixed_sum, grad_sum, weight_flat), None

    start = (jnp.zeros((TOKENS, D), jnp.float32), jnp.zeros((TOKENS, D), jnp.float32), jnp.zeros((assign_total,), jnp.float32))
    final, _ = lax.scan(per_expert, start, jnp.arange(EXPERTS, dtype=jnp.int32))
    mixed_sum, grad_sum, weight_flat = final
    return mixed_sum.astype(jnp.bfloat16), grad_sum.astype(jnp.bfloat16), weight_flat.reshape(TOKENS, TOPK)
```

```python
import functools

import jax
import jax.numpy as jnp
from jax import lax
from jax.experimental import pallas as pl
from jax.experimental.pallas import tpu as pltpu
from jax.sharding import PartitionSpec as P

MESH = pl.DeviceIdType.MESH
NT = (((1,), (1,)), ((), ()))
F32 = jnp.float32
BF16 = jnp.bfloat16


def ring_kernel(
    n,
    mean_length,
    seq_ref,
    tok_ref,
    cot_ref,
    ids_ref,
    rw_ref,
    gate_ref,
    up_ref,
    down_ref,
    mixed_ref,
    tgrad_ref,
    wgrad_ref,
    rows_in,
    out,
    pair_in,
    ring_in,
    w_send,
    w_in,
    w_col,
    g_send,
    g_in,
    ag_send,
    ag_recv,
    pair_send,
    pair_recv,
    op_send,
    op_recv,
    rs_send,
    rs_recv,
    w_sems,
    g_sems,
):
    rows, depth = tok_ref.shape
    top = ids_ref.shape[1]
    chips = n // 2
    half = chips // 2
    me = lax.axis_index("ctx")
    core = me % 2
    chip = me // 2
    side = chip % 2
    pos = (chip // 2) * (1 - side) + (chips - 1 - chip // 2) * side

    def device(back, plane):
        at = (pos + chips - back) % chips
        far = at // half
        other = 2 * (at * (1 - far) + (chips - 1 - at) * far) + far
        cc = core if plane == 0 else 1 - core
        return {"ctx": 2 * other + cc}

    def device_index(back, plane):
        return device(back, plane)["ctx"]

    right, left, partner = device(chips - 1, 0), device(1, 0), device(0, 1)
    peers = [(o, p) for o in range(chips) for p in range(2) if (o, p) != (0, 0)]

    barrier = pltpu.get_barrier_semaphore()
    for o, p in peers:
        pl.semaphore_signal(barrier, inc=1, device_id=device(o, p), device_id_type=MESH)

    rows_in[0, 0, 0:rows, :] = tok_ref[...]
    place = me * rows + lax.broadcasted_iota(jnp.int32, (rows, 128), 0)
    own_length = jnp.zeros((rows, 128), jnp.int32)
    begin = jnp.int32(0)
    for i in range(seq_ref.shape[0]):
        size = seq_ref[i]
        own_length = jnp.where((place >= begin) & (place < begin + size), size, own_length)
        begin = begin + size
    loss_weight = (mean_length / own_length.astype(F32))[:, 0:1]
    rows_in[1, 0, 0:rows, :] = (cot_ref[...].astype(F32) * loss_weight).astype(BF16)
    ids = ids_ref[...]
    weights = rw_ref[...]
    expert_lane = lax.broadcasted_iota(jnp.int32, (rows, 8 * n), 1) // 8
    by_expert = jnp.zeros((rows, 8 * n), F32)
    for k in range(top):
        by_expert = by_expert + jnp.where(ids[:, k : k + 1] == expert_lane, weights[:, k : k + 1], 0.0)
    w_send[...] = by_expert.T.reshape(n, 8, rows)

    pl.semaphore_wait(barrier, len(peers))

    def w_copy(o, p):
        return pltpu.make_async_remote_copy(
            src_ref=w_send.at[device_index(o, p)],
            dst_ref=w_in.at[2 * ((chips - o) % chips) + p],
            send_sem=w_sems.at[0],
            recv_sem=w_sems.at[1],
            device_id=device(o, p),
            device_id_type=MESH,
        )

    def ag_copy(a, src, dst, to):
        return pltpu.make_async_remote_copy(
            src_ref=rows_in.at[a, src, 0:rows],
            dst_ref=rows_in.at[a, dst, 0:rows],
            send_sem=ag_send.at[a, dst],
            recv_sem=ag_recv.at[a, dst],
            device_id=to,
            device_id_type=MESH,
        )

    def pair_copy(a, o):
        return pltpu.make_async_remote_copy(
            src_ref=rows_in.at[a, o, 0:rows],
            dst_ref=rows_in.at[a, o, rows : 2 * rows],
            send_sem=pair_send.at[a, o],
            recv_sem=pair_recv.at[a, o],
            device_id=partner,
            device_id_type=MESH,
        )

    def op_copy(a, o):
        return pltpu.make_async_remote_copy(
            src_ref=out.at[a, o, rows : 2 * rows],
            dst_ref=pair_in.at[a, o],
            send_sem=op_send.at[a, o],
            recv_sem=op_recv.at[a, o],
            device_id=partner,
            device_id_type=MESH,
        )

    def rs_copy(a, o, leftward):
        return pltpu.make_async_remote_copy(
            src_ref=out.at[a, o, 0:rows],
            dst_ref=ring_in.at[a, o - 1 if leftward else o + 1],
            send_sem=rs_send.at[a, o],
            recv_sem=rs_recv.at[a, o - 1 if leftward else o + 1],
            device_id=left if leftward else right,
            device_id_type=MESH,
        )

    def g_copy(o, p):
        return pltpu.make_async_remote_copy(
            src_ref=g_send.at[2 * o + p],
            dst_ref=g_in.at[me],
            send_sem=g_sems.at[0],
            recv_sem=g_sems.at[1],
            device_id=device(o, p),
            device_id_type=MESH,
        )

    for a in range(2):
        ag_copy(a, 0, 1, right).start()
        ag_copy(a, 0, chips - 1, left).start()
    for a in range(2):
        pair_copy(a, 0).start()
    for o, p in peers:
        w_copy(o, p).start()
    w_in[0] = w_send[me]

    def column(o, p):
        lane = lax.broadcasted_iota(jnp.int32, (rows, 8 * n), 1)
        return jnp.sum(jnp.where(lane == (2 * o + p) * 8, w_col[...], 0.0), axis=1, keepdims=True)

    def compute(o):
        x = rows_in[0, o]
        g = rows_in[1, o]
        weight = jnp.concatenate([column(o, 0), column(o, 1)], axis=0)
        gate_pre = jnp.dot(x, gate_ref[0], preferred_element_type=F32)
        up_value = jnp.dot(x, up_ref[0], preferred_element_type=F32)
        hidden_grad = lax.dot_general(g, down_ref[0], NT, preferred_element_type=F32)
        sig = 0.5 * jnp.tanh(0.5 * gate_pre) + 0.5
        act = gate_pre * sig
        hidden = act * up_value
        inner = (hidden * hidden_grad).astype(BF16)
        ones = jnp.ones((8, inner.shape[1]), BF16)
        inner_rows = lax.dot_general(ones, inner, NT, preferred_element_type=F32)
        g_send[2 * o] = inner_rows[:, 0:rows]
        g_send[2 * o + 1] = inner_rows[:, rows : 2 * rows]
        out[0, o] = jnp.dot(
            (hidden * weight).astype(BF16), down_ref[0], preferred_element_type=F32
        ).astype(BF16)
        scaled = hidden_grad * weight
        gate_grad = (scaled * up_value * (sig * (1.0 + gate_pre * (1.0 - sig)))).astype(BF16)
        up_grad = (scaled * act).astype(BF16)
        slot_grad = lax.dot_general(gate_grad, gate_ref[0], NT, preferred_element_type=F32)
        slot_grad = slot_grad + lax.dot_general(up_grad, up_ref[0], NT, preferred_element_type=F32)
        out[1, o] = slot_grad.astype(BF16)

    for a in range(2):
        pair_copy(a, 0).wait_recv()
    every_w = pltpu.make_async_copy(w_in.at[1:n], w_in.at[1:n], w_sems.at[1])
    every_w.wait()
    w_col[...] = w_in[...].reshape(8 * n, rows).T

    compute(0)
    for a in range(2):
        op_copy(a, 0).start()

    @pl.loop(1, half)
    def _(s):
        back = chips - s
        for a in range(2):
            ag_copy(a, s - 1, s, right).wait_recv()
            if a == 0:
                ag_copy(a, s, s + 1, right).start()
            else:
                @pl.when(s < half - 1)
                def _():
                    ag_copy(a, s, s + 1, right).start()
            pair_copy(a, s).start()
            ag_copy(a, s, back, left).wait_recv()
            if a == 1:
                ag_copy(a, back, back - 1, left).start()
            else:
                @pl.when(s < half - 1)
                def _():
                    ag_copy(a, back, back - 1, left).start()
            pair_copy(a, back).start()
        for a in range(2):
            pair_copy(a, s).wait_recv()
            pair_copy(a, back).wait_recv()

        @pl.loop(0, 2)
        def _(j):
            o = s * (1 - j) + back * j
            compute(o)
            for a in range(2):
                op_copy(a, o).start()

    def step(a, o, leftward, arrived):
        op_copy(a, o).wait_recv()
        total = out[a, o, 0:rows].astype(F32) + pair_in[a, o].astype(F32)
        if arrived:
            rs_copy(a, o + 1 if leftward else o - 1, leftward).wait_recv()
            total = total + ring_in[a, o].astype(F32)
        out[a, o, 0:rows] = total.astype(BF16)
        rs_copy(a, o, leftward).start()

    ag_copy(0, half - 1, half, right).wait_recv()
    pair_copy(0, half).start()
    ag_copy(1, half + 1, half, left).wait_recv()
    pair_copy(1, half).start()
    step(0, half + 1, False, False)
    step(1, half - 1, True, False)
    for a in range(2):
        pair_copy(a, half).wait_recv()
    compute(half)
    op_copy(1, half).start()
    op_copy(0, half).start()
    for o, p in peers:
        g_copy(o, p).start()
    g_in[me] = g_send[0]
    step(1, half, False, False)
    step(0, half, True, False)
    for d in range(1, half):
        if d + 1 < half:
            step(0, half + d + 1, False, True)
            step(1, half - d - 1, True, True)
        step(1, half + d, False, True)
        step(0, half - d, True, True)

    every_g = pltpu.make_async_copy(g_in.at[1:n], g_in.at[1:n], g_sems.at[1])
    every_g.wait()
    by_token = g_in[...].reshape(8 * n, rows).T
    lane = lax.broadcasted_iota(jnp.int32, (rows, 8 * n), 1)
    top_lane = lax.broadcasted_iota(jnp.int32, (rows, top), 1)
    picked = jnp.zeros((rows, top), F32)
    for k in range(top):
        value = jnp.sum(jnp.where(lane == ids[:, k : k + 1] * 8, by_token, 0.0), axis=1, keepdims=True)
        picked = jnp.where(top_lane == k, value, picked)
    wgrad_ref[...] = picked

    for a, result in ((0, mixed_ref), (1, tgrad_ref)):
        op_copy(a, 0).wait_recv()
        total = out[a, 0, 0:rows].astype(F32) + pair_in[a, 0].astype(F32)
        rs_copy(a, chips - 1, False).wait_recv()
        total = total + ring_in[a, chips].astype(F32)
        rs_copy(a, 1, True).wait_recv()
        total = total + ring_in[a, 0].astype(F32)
        result[...] = total.astype(BF16)

    for a in range(2):
        for s in range(1, chips):
            ag_copy(a, 0, s, right).wait_send()
            rs_copy(a, s, s < half).wait_send()
        for o in range(chips):
            pair_copy(a, o).wait_send()
            op_copy(a, o).wait_send()
    pltpu.make_async_copy(w_send.at[1:n], w_send.at[1:n], w_sems.at[0]).wait()
    pltpu.make_async_copy(g_send.at[1:n], g_send.at[1:n], g_sems.at[0]).wait()


def ring_device(tokens, cotangent, expert_ids, router_weights, seq_lengths, w_gate, w_up, w_down):
    n = lax.axis_size("ctx")
    chips = n // 2
    rows, depth = tokens.shape
    vmem = pl.BlockSpec(memory_space=pltpu.VMEM)
    dma = pltpu.SemaphoreType.DMA
    return pl.pallas_call(
        functools.partial(ring_kernel, n, rows * 4.0),
        out_shape=(
            jax.ShapeDtypeStruct(tokens.shape, BF16),
            jax.ShapeDtypeStruct(tokens.shape, BF16),
            jax.ShapeDtypeStruct(router_weights.shape, F32),
        ),
        in_specs=[pl.BlockSpec(memory_space=pltpu.SMEM)] + [vmem] * 7,
        out_specs=(vmem, vmem, vmem),
        scratch_shapes=[
            pltpu.VMEM((2, chips, 2 * rows, depth), BF16),
            pltpu.VMEM((2, chips, 2 * rows, depth), BF16),
            pltpu.VMEM((2, chips, rows, depth), BF16),
            pltpu.VMEM((2, chips + 1, rows, depth), BF16),
            pltpu.VMEM((n, 8, rows), F32),
            pltpu.VMEM((n, 8, rows), F32),
            pltpu.VMEM((rows, 8 * n), F32),
            pltpu.VMEM((n, 8, rows), F32),
            pltpu.VMEM((n, 8, rows), F32),
            dma((2, chips)),
            dma((2, chips)),
            dma((2, chips)),
            dma((2, chips)),
            dma((2, chips)),
            dma((2, chips)),
            dma((2, chips)),
            dma((2, chips + 1)),
            dma((2,)),
            dma((2,)),
        ],
        compiler_params=pltpu.CompilerParams(
            collective_id=0, has_side_effects=True, vmem_limit_bytes=52 * 1024 * 1024
        ),
        cost_estimate=pl.CostEstimate(
            flops=12 * n * rows * w_gate.size, bytes_accessed=6 * w_gate.size, transcendentals=0
        ),
    )(seq_lengths, tokens, cotangent, expert_ids, router_weights, w_gate, w_up, w_down)


def ring_fits(mesh, arrays):
    tokens, _, expert_ids, _, _, w_gate = arrays[:6]
    n = mesh.shape["ctx"]
    rows = tokens.shape[0] // (mesh.shape["groups"] * n * mesh.shape["dp"])
    held = 2 * n * rows * tokens.shape[1] * 2 * 4
    return (
        mesh.shape["dp"] == 1
        and w_gate.shape[0] == n
        and n % 4 == 0
        and n >= 8
        and rows % 128 == 0
        and held <= 40 * 1024 * 1024
    )


def loss_scale(position, seq_lengths, mean_length):
    ends = jnp.cumsum(seq_lengths)
    starts = ends - seq_lengths
    inside = (position[:, None] >= starts[None, :]) & (position[:, None] < ends[None, :])
    own_length = jnp.sum(jnp.where(inside, seq_lengths[None, :], 0), axis=1)
    return mean_length / own_length.astype(jnp.float32)


def forward_rows(slot_rows, gate_full, up_full, down_full):
    gate_pre = jnp.dot(slot_rows, gate_full, preferred_element_type=jnp.float32)
    up_value = jnp.dot(slot_rows, up_full, preferred_element_type=jnp.float32)
    activated = jax.nn.silu(gate_pre)
    hidden = (activated * up_value).astype(jnp.bfloat16)
    expert_out = jnp.dot(hidden, down_full, preferred_element_type=jnp.float32).astype(jnp.bfloat16)
    return (gate_pre, up_value, activated, expert_out)


def backward_rows(grad_rows, gate_pre, up_value, activated, gate_full, up_full, down_full):
    contract = (((1,), (1,)), ((), ()))
    hidden_grad = lax.dot_general(
        grad_rows, down_full, contract, preferred_element_type=jnp.float32
    )
    sigmoid_value = jax.nn.sigmoid(gate_pre)
    silu_slope = sigmoid_value * (1.0 + gate_pre * (1.0 - sigmoid_value))
    gate_grad = (hidden_grad * up_value * silu_slope).astype(jnp.bfloat16)
    up_grad = (hidden_grad * activated).astype(jnp.bfloat16)
    slot_grad = lax.dot_general(gate_grad, gate_full, contract, preferred_element_type=jnp.float32)
    slot_grad = slot_grad + lax.dot_general(
        up_grad, up_full, contract, preferred_element_type=jnp.float32
    )
    return slot_grad.astype(jnp.bfloat16)


def slot_ranks(flat_ids, experts):
    expert_hits = (flat_ids[:, None] == jnp.arange(experts, dtype=jnp.int32)[None, :]).astype(
        jnp.int32
    )
    assign_count = flat_ids.shape[0]
    row_iota = lax.broadcasted_iota(jnp.int32, (assign_count, assign_count), 0)
    col_iota = lax.broadcasted_iota(jnp.int32, (assign_count, assign_count), 1)
    lower_mask = (row_iota > col_iota).astype(jnp.bfloat16)
    earlier = jnp.dot(
        lower_mask, expert_hits.astype(jnp.bfloat16), preferred_element_type=jnp.float32
    )
    return jnp.sum(earlier * expert_hits.astype(jnp.float32), axis=1).astype(jnp.int32)


def per_device(tokens, cotangent, expert_ids, router_weights, seq_lengths, w_gate, w_up, w_down):
    ctx_count = lax.axis_size("ctx")
    dp_count = lax.axis_size("dp")
    row_count, top_count = expert_ids.shape
    slot_cap = max(2, min(row_count, row_count * top_count * 5 // (4 * ctx_count)))
    block_index = lax.axis_index("ctx") * dp_count + lax.axis_index("dp")
    position = block_index * row_count + jnp.arange(row_count, dtype=jnp.int32)
    loss_weight = loss_scale(position, seq_lengths, row_count * 4.0)
    out_grad = (cotangent.astype(jnp.float32) * loss_weight[:, None]).astype(jnp.bfloat16)
    flat_ids = expert_ids.reshape(-1)
    assign_count = flat_ids.shape[0]
    dest_slot = flat_ids * slot_cap + slot_ranks(flat_ids, ctx_count)
    source_row = jnp.full((ctx_count * slot_cap,), assign_count, jnp.int32)
    source_row = source_row.at[dest_slot].set(jnp.arange(assign_count, dtype=jnp.int32))
    filled = source_row < assign_count
    token_of = jnp.minimum(source_row, assign_count - 1) // top_count
    zero_value = jnp.zeros((), jnp.bfloat16)
    token_send = jnp.where(filled[:, None], tokens[token_of], zero_value).reshape(
        ctx_count, slot_cap, -1
    )
    grad_send = jnp.where(filled[:, None], out_grad[token_of], zero_value).reshape(
        ctx_count, slot_cap, -1
    )
    gate_full, up_full, down_full = (
        lax.all_gather(w_gate[0], "dp", axis=0, tiled=True),
        lax.all_gather(w_up[0], "dp", axis=0, tiled=True),
        lax.all_gather(w_down[0], "dp", axis=1, tiled=True),
    )
    token_arrived = lax.all_to_all(token_send, "ctx", split_axis=0, concat_axis=0, tiled=True)
    grad_arrived = lax.all_to_all(grad_send, "ctx", split_axis=0, concat_axis=0, tiled=True)
    source_count = token_arrived.shape[0]
    slot_count = token_arrived.shape[1]
    slot_rows = token_arrived.reshape(source_count * slot_count, -1)
    grad_rows = grad_arrived.reshape(source_count * slot_count, -1)
    gate_pre, up_value, activated, expert_out = forward_rows(
        slot_rows, gate_full, up_full, down_full
    )
    out_blocks = expert_out.reshape(source_count, slot_count, -1)
    slot_grad = backward_rows(
        grad_rows, gate_pre, up_value, activated, gate_full, up_full, down_full
    )
    out_home = lax.all_to_all(out_blocks, "ctx", split_axis=0, concat_axis=0, tiled=True)
    grad_home = lax.all_to_all(
        slot_grad.reshape(source_count, slot_count, -1),
        "ctx",
        split_axis=0,
        concat_axis=0,
        tiled=True,
    )
    out_rows = out_home.reshape(ctx_count * slot_cap, -1)[dest_slot].reshape(
        row_count, top_count, -1
    )
    grad_rows = grad_home.reshape(ctx_count * slot_cap, -1)[dest_slot].reshape(
        row_count, top_count, -1
    )
    mixed = jnp.sum(router_weights[:, :, None] * out_rows.astype(jnp.float32), axis=1).astype(
        jnp.bfloat16
    )
    token_grads = jnp.sum(
        router_weights[:, :, None] * grad_rows.astype(jnp.float32), axis=1
    ).astype(jnp.bfloat16)
    weight_grads = jnp.einsum("td,tkd->tk", out_grad, out_rows, preferred_element_type=jnp.float32)
    return (mixed, token_grads, weight_grads)


def solution(mesh):
    in_specs = (
        P(("groups", "ctx", "dp"), None),
        P(("groups", "ctx", "dp"), None),
        P(("groups", "ctx", "dp"), None),
        P(("groups", "ctx", "dp"), None),
        P("groups"),
        P("ctx", "dp", None),
        P("ctx", "dp", None),
        P("ctx", None, "dp"),
    )
    out_specs = (
        P(("groups", "ctx", "dp"), None),
        P(("groups", "ctx", "dp"), None),
        P(("groups", "ctx", "dp"), None),
    )

    def run(*arrays):
        plan = ring_device if ring_fits(mesh, arrays) else per_device
        return jax.shard_map(
            plan, mesh=mesh, in_specs=in_specs, out_specs=out_specs, check_vma=False
        )(*arrays)

    return run
```

```python
import functools

import jax
import jax.numpy as jnp
from jax import lax
from jax.experimental import pallas as pl
from jax.experimental.pallas import tpu as pltpu
from jax.sharding import PartitionSpec as P

MESH = pl.DeviceIdType.MESH
NT = (((1,), (1,)), ((), ()))
F32 = jnp.float32
BF16 = jnp.bfloat16


def line_kernel(
    n,
    mean_length,
    seq_ref,
    tok_ref,
    cot_ref,
    ids_ref,
    rw_ref,
    gate_hbm,
    up_hbm,
    down_hbm,
    mixed_ref,
    tgrad_ref,
    wgrad_ref,
    gate_ref,
    up_ref,
    down_ref,
    rows_in,
    acc,
    out,
    pair_in,
    line_in,
    w_send,
    w_in,
    w_col,
    g_send,
    g_in,
    load_sems,
    x_send,
    x_recv,
    y_send,
    y_recv,
    ag_send,
    ag_recv,
    pair_send,
    pair_recv,
    op_send,
    op_recv,
    rs_send,
    rs_recv,
    w_sems,
    g_sems,
):
    rows, depth = tok_ref.shape
    top = ids_ref.shape[0]
    planes = n // 4
    me = lax.axis_index("ctx")
    group = lax.axis_index("groups")
    core = me % 2
    side = (me // 2) % 2
    z = me // 4

    def at(zz, plane):
        cc = core if plane == 0 else 1 - core
        return {"groups": group, "ctx": (zz * 2 + side) * 2 + cc}

    partner = at(z, 1)
    x_mate = {"groups": group, "ctx": (z * 2 + 1 - side) * 2 + core}
    y_mate = {"groups": 1 - group, "ctx": me}
    above, below = at((z + 1) % planes, 0), at((z + planes - 1) % planes, 0)
    line = [(d, p) for d in range(planes) for p in range(2) if (d, p) != (0, 0)]

    barrier = pltpu.get_barrier_semaphore()
    for to in [at((z + d) % planes, p) for d, p in line] + [x_mate, y_mate]:
        pl.semaphore_signal(barrier, inc=1, device_id=to, device_id_type=MESH)

    parts = ((gate_hbm, gate_ref), (up_hbm, up_ref), (down_hbm, down_ref))
    loads = [
        pltpu.make_async_copy(src.at[0], dst.at[0], load_sems.at[i])
        for i, (src, dst) in enumerate(parts)
    ]
    for load in loads:
        load.start()

    rows_in[0, z, 0:rows, :] = tok_ref[...]
    place = me * rows + lax.broadcasted_iota(jnp.int32, (rows, 128), 0)
    own_length = jnp.zeros((rows, 128), jnp.int32)
    begin = jnp.int32(0)
    for i in range(seq_ref.shape[0]):
        size = seq_ref[i]
        own_length = jnp.where((place >= begin) & (place < begin + size), size, own_length)
        begin = begin + size
    loss_weight = (mean_length / own_length.astype(F32))[:, 0:1]
    rows_in[1, z, 0:rows, :] = (cot_ref[...].astype(F32) * loss_weight).astype(BF16)

    pl.semaphore_wait(barrier, len(line) + 2)

    def ag_copy(a, slot, to):
        return pltpu.make_async_remote_copy(
            src_ref=rows_in.at[a, slot, 0:rows],
            dst_ref=rows_in.at[a, slot, 0:rows],
            send_sem=ag_send.at[a, slot, 0 if to is above else 1],
            recv_sem=ag_recv.at[a, slot],
            device_id=to,
            device_id_type=MESH,
        )

    def pair_copy(a, slot):
        return pltpu.make_async_remote_copy(
            src_ref=rows_in.at[a, slot, 0:rows],
            dst_ref=rows_in.at[a, slot, rows : 2 * rows],
            send_sem=pair_send.at[a, slot],
            recv_sem=pair_recv.at[a, slot],
            device_id=partner,
            device_id_type=MESH,
        )

    def op_copy(a, slot):
        return pltpu.make_async_remote_copy(
            src_ref=out.at[a, slot, rows : 2 * rows],
            dst_ref=pair_in.at[a, slot],
            send_sem=op_send.at[a, slot],
            recv_sem=op_recv.at[a, slot],
            device_id=partner,
            device_id_type=MESH,
        )

    def rs_copy(a, slot, arrive, to):
        return pltpu.make_async_remote_copy(
            src_ref=out.at[a, slot, 0:rows],
            dst_ref=line_in.at[a, arrive],
            send_sem=rs_send.at[a, slot],
            recv_sem=rs_recv.at[a, arrive],
            device_id=to,
            device_id_type=MESH,
        )

    def half_of(i, which):
        count = parts[i][1].shape[1] // 2
        return pl.ds(pl.multiple_of(which * count, count), count)

    def x_copy(i):
        return pltpu.make_async_remote_copy(
            src_ref=parts[i][0].at[0, half_of(i, group)],
            dst_ref=parts[i][1].at[1, half_of(i, group)],
            send_sem=x_send.at[i],
            recv_sem=x_recv.at[i],
            device_id=x_mate,
            device_id_type=MESH,
        )

    def y_copy(i):
        return pltpu.make_async_remote_copy(
            src_ref=parts[i][1].at[1, half_of(i, group)],
            dst_ref=parts[i][1].at[1, half_of(i, group)],
            send_sem=y_send.at[i],
            recv_sem=y_recv.at[i],
            device_id=y_mate,
            device_id_type=MESH,
        )

    def w_copy(d, p):
        there = (z + d) % planes
        return pltpu.make_async_remote_copy(
            src_ref=w_send.at[2 * there + (core if p == 0 else 1 - core)],
            dst_ref=w_in.at[2 * z + p],
            send_sem=w_sems.at[0],
            recv_sem=w_sems.at[1],
            device_id=at(there, p),
            device_id_type=MESH,
        )

    def g_copy(d, p):
        there = (z + d) % planes
        return pltpu.make_async_remote_copy(
            src_ref=g_send.at[2 * there + p],
            dst_ref=g_in.at[2 * z + core],
            send_sem=g_sems.at[0],
            recv_sem=g_sems.at[1],
            device_id=at(there, p),
            device_id_type=MESH,
        )

    def send_on(a, slot, upward):
        if upward:
            @pl.when(z < planes - 1)
            def _():
                ag_copy(a, slot, above).start()
        else:
            @pl.when(z > 0)
            def _():
                ag_copy(a, slot, below).start()

    for a in range(2):
        send_on(a, z, True)
        send_on(a, z, False)
    for i in range(3):
        x_copy(i).start()
    for a in range(2):
        pair_copy(a, z).start()

    shape = (8 * n, rows)
    place_of = lax.broadcasted_iota(jnp.int32, shape, 0) // 8
    expert_of = (place_of // 4 * 2 + place_of % 2) * 2 + place_of // 2 % 2
    by_expert = jnp.zeros(shape, F32)
    for k in range(top):
        by_expert = by_expert + jnp.where(ids_ref[k : k + 1, :] == expert_of, rw_ref[k : k + 1, :], 0.0)
    w_send[...] = by_expert.reshape(n // 2, 2, 8, rows)
    for d, p in line:
        w_copy(d, p).start()
    w_in[2 * z] = w_send[2 * z + core]

    for load in loads:
        load.wait()
    for a in range(2):
        pair_copy(a, z).wait_recv()
    every = w_in.at[1 : 2 * planes]
    pltpu.make_async_copy(every, every, w_sems.at[1]).wait()
    w_col[...] = w_in[...].reshape(8 * n, rows).T

    def column(slot, p, whose):
        lane = lax.broadcasted_iota(jnp.int32, (rows, 8 * n), 1)
        wanted = ((2 * slot + p) * 2 + whose) * 8
        return jnp.sum(jnp.where(lane == wanted, w_col[...], 0.0), axis=1, keepdims=True)

    def compute(e, slot):
        whose = side if e == 0 else 1 - side
        x = rows_in[0, slot]
        g = rows_in[1, slot]
        weight = jnp.concatenate([column(slot, 0, whose), column(slot, 1, whose)], axis=0)
        gate_pre = jnp.dot(x, gate_ref[e], preferred_element_type=F32)
        up_value = jnp.dot(x, up_ref[e], preferred_element_type=F32)
        hidden_grad = lax.dot_general(g, down_ref[e], NT, preferred_element_type=F32)
        sig = 0.5 * jnp.tanh(0.5 * gate_pre) + 0.5
        act = gate_pre * sig
        hidden = act * up_value
        inner = (hidden * hidden_grad).astype(BF16)
        ones = jnp.ones((8, inner.shape[1]), BF16)
        inner_rows = lax.dot_general(ones, inner, NT, preferred_element_type=F32)
        g_send[2 * slot, whose] = inner_rows[:, 0:rows]
        g_send[2 * slot + 1, whose] = inner_rows[:, rows : 2 * rows]
        mix = jnp.dot((hidden * weight).astype(BF16), down_ref[e], preferred_element_type=F32)
        scaled = hidden_grad * weight
        gate_grad = (scaled * up_value * (sig * (1.0 + gate_pre * (1.0 - sig)))).astype(BF16)
        up_grad = (scaled * act).astype(BF16)
        slot_grad = lax.dot_general(gate_grad, gate_ref[e], NT, preferred_element_type=F32)
        slot_grad = slot_grad + lax.dot_general(up_grad, up_ref[e], NT, preferred_element_type=F32)
        if e == 0:
            acc[0, slot] = mix
            acc[1, slot] = slot_grad
        else:
            out[0, slot] = (acc[0, slot] + mix).astype(BF16)
            out[1, slot] = (acc[1, slot] + slot_grad).astype(BF16)
            for a in range(2):
                op_copy(a, slot).start()

    def arrivals(s):
        for a in range(2):
            @pl.when(z - s >= 0)
            def _():
                ag_copy(a, z - s, above).wait_recv()
                send_on(a, z - s, True)
                pair_copy(a, z - s).start()

            @pl.when(z + s < planes)
            def _():
                ag_copy(a, z + s, below).wait_recv()
                send_on(a, z + s, False)
                pair_copy(a, z + s).start()

    def first_pass(s):
        @pl.loop(0, 2)
        def _(j):
            slot = z - s + 2 * s * j

            @pl.when((slot >= 0) & (slot < planes))
            def _():
                for a in range(2):
                    pair_copy(a, slot).wait_recv()
                compute(0, slot)

    def pass_on(i):
        x_copy(i).wait_recv()
        y_copy(i).start()

    def line_step(dest, upward, wanted):
        first = 0 if upward else planes - 1

        def send(a):
            if upward:
                @pl.when(z + 1 == dest)
                def _():
                    rs_copy(a, dest, planes, above).start()

                @pl.when(z + 1 != dest)
                def _():
                    rs_copy(a, dest, dest, above).start()
            else:
                rs_copy(a, dest, dest, below).start()

        def add(a, arrived):
            op_copy(a, dest).wait_recv()
            total = out[a, dest, 0:rows].astype(F32) + pair_in[a, dest].astype(F32)
            if arrived:
                rs_copy(a, dest, dest, above).wait_recv()
                total = total + line_in[a, dest].astype(F32)
            out[a, dest, 0:rows] = total.astype(BF16)
            send(a)

        @pl.when(wanted & (z < dest if upward else z > dest))
        def _():
            @pl.when(z != first)
            def _():
                for a in range(2):
                    add(a, True)

            @pl.when(z == first)
            def _():
                for a in range(2):
                    add(a, False)

    upward = [planes - 2, planes - 1] + list(range(planes - 3, 0, -1))
    table = []
    for zz in range(planes):
        low = zz < planes // 2
        order = [u if low else planes - 1 - u for u in upward + [0]]
        table.append([u for u in order if u != zz] + [zz])

    def turn(k):
        slot = 0
        for zz in range(planes):
            slot = slot + table[zz][k] * (z == zz).astype(jnp.int32)
        return slot

    compute(0, z)
    last = planes - 1
    for s in range(1, last):
        arrivals(s)
        if s <= 2:
            pass_on(s - 1)
        first_pass(s)
    pass_on(2)
    for i in range(3):
        y_copy(i).wait_recv()
    compute(1, turn(0))
    arrivals(last)
    inner = (z > 0) & (z < last)
    high = z >= planes // 2
    for k, u in enumerate(upward):
        line_step(planes - 1 - u, False, high)
        line_step(u, True, z >= 0)
        line_step(planes - 1 - u, False, z < planes // 2)
        if k == 0:
            first_pass(last)

            @pl.loop(1, 4)
            def _(j):
                slot = 0
                for jj in range(1, 4):
                    slot = slot + turn(jj) * (j == jj).astype(jnp.int32)

                @pl.when((j < 3) | inner)
                def _():
                    compute(1, slot)
        elif k == 1:
            @pl.when((z == 0) | (z == last))
            def _():
                compute(1, turn(3))
        elif k + 2 < planes:
            compute(1, turn(k + 2))
    for d, p in line:
        g_copy(d, p).start()
    g_in[2 * z + core] = g_send[2 * z]

    every = g_in.at[1 : 2 * planes]
    pltpu.make_async_copy(every, every, g_sems.at[1]).wait()
    ids = ids_ref[...]
    picked = jnp.zeros((top, rows), F32)
    for e in range(n):
        picked = jnp.where(ids == e, g_in[e // 4 * 2 + e % 2, e // 2 % 2][0:top], picked)
    wgrad_ref[...] = picked

    for a in range(2):
        op_copy(a, z).wait_recv()
        total = out[a, z, 0:rows].astype(F32) + pair_in[a, z].astype(F32)
        acc[a, z, 0:rows] = total

        @pl.when(z > 0)
        def _():
            rs_copy(a, z, planes, above).wait_recv()
            acc[a, z, 0:rows] = acc[a, z, 0:rows] + line_in[a, planes].astype(F32)

        @pl.when(z < planes - 1)
        def _():
            rs_copy(a, z, z, below).wait_recv()
            acc[a, z, 0:rows] = acc[a, z, 0:rows] + line_in[a, z].astype(F32)

    mixed_ref[...] = acc[0, z, 0:rows].astype(BF16)
    tgrad_ref[...] = acc[1, z, 0:rows].astype(BF16)

    for a in range(2):
        for slot in range(planes):
            @pl.when((slot <= z) & (z < planes - 1))
            def _():
                ag_copy(a, slot, above).wait_send()

            @pl.when((slot >= z) & (z > 0))
            def _():
                ag_copy(a, slot, below).wait_send()

            @pl.when(slot != z)
            def _():
                rs_copy(a, slot, slot, above).wait_send()

            pair_copy(a, slot).wait_send()
            op_copy(a, slot).wait_send()
    for i in range(3):
        x_copy(i).wait_send()
        y_copy(i).wait_send()
    every = w_send.at[1 : 2 * planes]
    pltpu.make_async_copy(every, every, w_sems.at[0]).wait()
    every = g_send.at[1 : 2 * planes]
    pltpu.make_async_copy(every, every, g_sems.at[0]).wait()


def line_device(tokens, cotangent, expert_ids, router_weights, seq_lengths, w_gate, w_up, w_down):
    n = lax.axis_size("ctx")
    planes = n // 4
    rows, depth = tokens.shape
    hidden = w_gate.shape[2]
    top = expert_ids.shape[1]
    vmem = pl.BlockSpec(memory_space=pltpu.VMEM)
    hbm = pl.BlockSpec(memory_space=pl.ANY)
    dma = pltpu.SemaphoreType.DMA
    mixed, token_grads, weight_grads = pl.pallas_call(
        functools.partial(line_kernel, n, rows * 4.0),
        out_shape=(
            jax.ShapeDtypeStruct(tokens.shape, BF16),
            jax.ShapeDtypeStruct(tokens.shape, BF16),
            jax.ShapeDtypeStruct((top, rows), F32),
        ),
        in_specs=[pl.BlockSpec(memory_space=pltpu.SMEM)] + [vmem] * 4 + [hbm] * 3,
        out_specs=(vmem, vmem, vmem),
        scratch_shapes=[
            pltpu.VMEM((2, depth, hidden), BF16),
            pltpu.VMEM((2, depth, hidden), BF16),
            pltpu.VMEM((2, hidden, depth), BF16),
            pltpu.VMEM((2, planes, 2 * rows, depth), BF16),
            pltpu.VMEM((2, planes, 2 * rows, depth), F32),
            pltpu.VMEM((2, planes, 2 * rows, depth), BF16),
            pltpu.VMEM((2, planes, rows, depth), BF16),
            pltpu.VMEM((2, planes + 1, rows, depth), BF16),
            pltpu.VMEM((n // 2, 2, 8, rows), F32),
            pltpu.VMEM((n // 2, 2, 8, rows), F32),
            pltpu.VMEM((rows, 8 * n), F32),
            pltpu.VMEM((n // 2, 2, 8, rows), F32),
            pltpu.VMEM((n // 2, 2, 8, rows), F32),
            dma((3,)),
            dma((3,)),
            dma((3,)),
            dma((3,)),
            dma((3,)),
            dma((2, planes, 2)),
            dma((2, planes)),
            dma((2, planes)),
            dma((2, planes)),
            dma((2, planes)),
            dma((2, planes)),
            dma((2, planes)),
            dma((2, planes + 1)),
            dma((2,)),
            dma((2,)),
        ],
        compiler_params=pltpu.CompilerParams(
            collective_id=0, has_side_effects=True, vmem_limit_bytes=52 * 1024 * 1024
        ),
        cost_estimate=pl.CostEstimate(
            flops=12 * n * rows * w_gate.size, bytes_accessed=6 * w_gate.size, transcendentals=0
        ),
    )(seq_lengths, tokens, cotangent, expert_ids.T, router_weights.T, w_gate, w_up, w_down)
    return mixed, token_grads, weight_grads.T


def line_fits(mesh, arrays):
    tokens, _, expert_ids, _, _, w_gate = arrays[:6]
    n = mesh.shape["ctx"]
    rows = tokens.shape[0] // (mesh.shape["groups"] * n * mesh.shape["dp"])
    held = 2 * n * rows * tokens.shape[1] * 9
    return (
        mesh.shape["dp"] == 1
        and mesh.shape["groups"] == 2
        and w_gate.shape[0] == n
        and w_gate.shape[1] % 32 == 0
        and w_gate.shape[2] % 32 == 0
        and n % 8 == 0
        and n >= 16
        and expert_ids.shape[1] <= 8
        and rows % 128 == 0
        and held <= 40 * 1024 * 1024
    )


def loss_scale(position, seq_lengths, mean_length):
    ends = jnp.cumsum(seq_lengths)
    starts = ends - seq_lengths
    inside = (position[:, None] >= starts[None, :]) & (position[:, None] < ends[None, :])
    own_length = jnp.sum(jnp.where(inside, seq_lengths[None, :], 0), axis=1)
    return mean_length / own_length.astype(jnp.float32)


def forward_rows(slot_rows, gate_full, up_full, down_full):
    gate_pre = jnp.dot(slot_rows, gate_full, preferred_element_type=jnp.float32)
    up_value = jnp.dot(slot_rows, up_full, preferred_element_type=jnp.float32)
    activated = jax.nn.silu(gate_pre)
    hidden = (activated * up_value).astype(jnp.bfloat16)
    expert_out = jnp.dot(hidden, down_full, preferred_element_type=jnp.float32).astype(jnp.bfloat16)
    return (gate_pre, up_value, activated, expert_out)


def backward_rows(grad_rows, gate_pre, up_value, activated, gate_full, up_full, down_full):
    contract = (((1,), (1,)), ((), ()))
    hidden_grad = lax.dot_general(
        grad_rows, down_full, contract, preferred_element_type=jnp.float32
    )
    sigmoid_value = jax.nn.sigmoid(gate_pre)
    silu_slope = sigmoid_value * (1.0 + gate_pre * (1.0 - sigmoid_value))
    gate_grad = (hidden_grad * up_value * silu_slope).astype(jnp.bfloat16)
    up_grad = (hidden_grad * activated).astype(jnp.bfloat16)
    slot_grad = lax.dot_general(gate_grad, gate_full, contract, preferred_element_type=jnp.float32)
    slot_grad = slot_grad + lax.dot_general(
        up_grad, up_full, contract, preferred_element_type=jnp.float32
    )
    return slot_grad.astype(jnp.bfloat16)


def slot_ranks(flat_ids, experts):
    expert_hits = (flat_ids[:, None] == jnp.arange(experts, dtype=jnp.int32)[None, :]).astype(
        jnp.int32
    )
    assign_count = flat_ids.shape[0]
    row_iota = lax.broadcasted_iota(jnp.int32, (assign_count, assign_count), 0)
    col_iota = lax.broadcasted_iota(jnp.int32, (assign_count, assign_count), 1)
    lower_mask = (row_iota > col_iota).astype(jnp.bfloat16)
    earlier = jnp.dot(
        lower_mask, expert_hits.astype(jnp.bfloat16), preferred_element_type=jnp.float32
    )
    return jnp.sum(earlier * expert_hits.astype(jnp.float32), axis=1).astype(jnp.int32)


def per_device(tokens, cotangent, expert_ids, router_weights, seq_lengths, w_gate, w_up, w_down):
    ctx_count = lax.axis_size("ctx")
    dp_count = lax.axis_size("dp")
    row_count, top_count = expert_ids.shape
    slot_cap = max(2, min(row_count, row_count * top_count * 5 // (4 * ctx_count)))
    block_index = lax.axis_index("ctx") * dp_count + lax.axis_index("dp")
    position = block_index * row_count + jnp.arange(row_count, dtype=jnp.int32)
    loss_weight = loss_scale(position, seq_lengths, row_count * 4.0)
    out_grad = (cotangent.astype(jnp.float32) * loss_weight[:, None]).astype(jnp.bfloat16)
    flat_ids = expert_ids.reshape(-1)
    assign_count = flat_ids.shape[0]
    dest_slot = flat_ids * slot_cap + slot_ranks(flat_ids, ctx_count)
    source_row = jnp.full((ctx_count * slot_cap,), assign_count, jnp.int32)
    source_row = source_row.at[dest_slot].set(jnp.arange(assign_count, dtype=jnp.int32))
    filled = source_row < assign_count
    token_of = jnp.minimum(source_row, assign_count - 1) // top_count
    zero_value = jnp.zeros((), jnp.bfloat16)
    token_send = jnp.where(filled[:, None], tokens[token_of], zero_value).reshape(
        ctx_count, slot_cap, -1
    )
    grad_send = jnp.where(filled[:, None], out_grad[token_of], zero_value).reshape(
        ctx_count, slot_cap, -1
    )
    gate_full, up_full, down_full = (
        lax.all_gather(w_gate[0], "dp", axis=0, tiled=True),
        lax.all_gather(w_up[0], "dp", axis=0, tiled=True),
        lax.all_gather(w_down[0], "dp", axis=1, tiled=True),
    )
    token_arrived = lax.all_to_all(token_send, "ctx", split_axis=0, concat_axis=0, tiled=True)
    grad_arrived = lax.all_to_all(grad_send, "ctx", split_axis=0, concat_axis=0, tiled=True)
    source_count = token_arrived.shape[0]
    slot_count = token_arrived.shape[1]
    slot_rows = token_arrived.reshape(source_count * slot_count, -1)
    grad_rows = grad_arrived.reshape(source_count * slot_count, -1)
    gate_pre, up_value, activated, expert_out = forward_rows(
        slot_rows, gate_full, up_full, down_full
    )
    out_blocks = expert_out.reshape(source_count, slot_count, -1)
    slot_grad = backward_rows(
        grad_rows, gate_pre, up_value, activated, gate_full, up_full, down_full
    )
    out_home = lax.all_to_all(out_blocks, "ctx", split_axis=0, concat_axis=0, tiled=True)
    grad_home = lax.all_to_all(
        slot_grad.reshape(source_count, slot_count, -1),
        "ctx",
        split_axis=0,
        concat_axis=0,
        tiled=True,
    )
    out_rows = out_home.reshape(ctx_count * slot_cap, -1)[dest_slot].reshape(
        row_count, top_count, -1
    )
    grad_rows = grad_home.reshape(ctx_count * slot_cap, -1)[dest_slot].reshape(
        row_count, top_count, -1
    )
    mixed = jnp.sum(router_weights[:, :, None] * out_rows.astype(jnp.float32), axis=1).astype(
        jnp.bfloat16
    )
    token_grads = jnp.sum(
        router_weights[:, :, None] * grad_rows.astype(jnp.float32), axis=1
    ).astype(jnp.bfloat16)
    weight_grads = jnp.einsum("td,tkd->tk", out_grad, out_rows, preferred_element_type=jnp.float32)
    return (mixed, token_grads, weight_grads)


def solution(mesh):
    in_specs = (
        P(("groups", "ctx", "dp"), None),
        P(("groups", "ctx", "dp"), None),
        P(("groups", "ctx", "dp"), None),
        P(("groups", "ctx", "dp"), None),
        P("groups"),
        P("ctx", "dp", None),
        P("ctx", "dp", None),
        P("ctx", None, "dp"),
    )
    out_specs = (
        P(("groups", "ctx", "dp"), None),
        P(("groups", "ctx", "dp"), None),
        P(("groups", "ctx", "dp"), None),
    )

    def run(*arrays):
        plan = line_device if line_fits(mesh, arrays) else per_device
        return jax.shard_map(
            plan, mesh=mesh, in_specs=in_specs, out_specs=out_specs, check_vma=False
        )(*arrays)

    return run
```

```python
import functools

import jax
import jax.numpy as jnp
from jax import lax
from jax.experimental import pallas as pl
from jax.experimental.pallas import tpu as pltpu
from jax.sharding import PartitionSpec as P

MESH = pl.DeviceIdType.MESH
NT = (((1,), (1,)), ((), ()))
F32 = jnp.float32
BF16 = jnp.bfloat16


def line_kernel(
    n,
    mean_length,
    seq_ref,
    tok_hbm,
    cot_hbm,
    ids_ref,
    rw_ref,
    gate_hbm,
    up_hbm,
    down_hbm,
    mixed_ref,
    tgrad_ref,
    wgrad_ref,
    both_ref,
    down_ref,
    cot_ref,
    rows_in,
    acc,
    out,
    pair_in,
    line_in,
    w_send,
    w_in,
    w_col,
    g_send,
    g_in,
    load_sems,
    x_send,
    x_recv,
    y_send,
    y_recv,
    ag_send,
    ag_recv,
    pair_send,
    pair_recv,
    op_send,
    op_recv,
    rs_send,
    rs_recv,
    w_sems,
    g_sems,
):
    rows, depth = tok_hbm.shape
    wide = gate_hbm.shape[2]
    top = ids_ref.shape[0]
    planes = n // 4
    me = lax.axis_index("ctx")
    group = lax.axis_index("groups")
    core = me % 2
    side = (me // 2) % 2
    z = me // 4

    def at(zz, plane):
        cc = core if plane == 0 else 1 - core
        return {"groups": group, "ctx": (zz * 2 + side) * 2 + cc}

    partner = at(z, 1)
    x_mate = {"groups": group, "ctx": (z * 2 + 1 - side) * 2 + core}
    y_mate = {"groups": 1 - group, "ctx": me}
    above, below = at((z + 1) % planes, 0), at((z + planes - 1) % planes, 0)
    line = [(d, p) for d in range(planes) for p in range(2) if (d, p) != (0, 0)]

    barrier = pltpu.get_barrier_semaphore()
    for to in [at((z + d) % planes, p) for d, p in line] + [x_mate, y_mate]:
        pl.semaphore_signal(barrier, inc=1, device_id=to, device_id_type=MESH)

    sources = (gate_hbm, up_hbm, down_hbm)

    def weight_ref(i, e, place):
        if i == 2:
            return down_ref.at[e, place]
        return both_ref.at[e, place, i * wide : (i + 1) * wide]

    inputs = (
        (cot_hbm, cot_ref),
        (tok_hbm, rows_in.at[0, z, 0:rows]),
    ) + tuple(
        (sources[i].at[0], weight_ref(i, 0, pl.ds(0, sources[i].shape[1]))) for i in range(3)
    )
    loads = [
        pltpu.make_async_copy(src, dst, load_sems.at[i]) for i, (src, dst) in enumerate(inputs)
    ]
    for load in loads:
        load.start()

    place = me * rows + lax.broadcasted_iota(jnp.int32, (rows, 128), 0)
    own_length = jnp.zeros((rows, 128), jnp.int32)
    begin = jnp.int32(0)
    for i in range(seq_ref.shape[0]):
        size = seq_ref[i]
        own_length = jnp.where((place >= begin) & (place < begin + size), size, own_length)
        begin = begin + size
    loss_weight = (mean_length / own_length.astype(F32))[:, 0:1]
    loads[0].wait()
    rows_in[1, z, 0:rows, :] = (cot_ref[...].astype(F32) * loss_weight).astype(BF16)

    loads[1].wait()
    pl.semaphore_wait(barrier, len(line) + 2)

    def ag_copy(a, slot, to):
        return pltpu.make_async_remote_copy(
            src_ref=rows_in.at[a, slot, 0:rows],
            dst_ref=rows_in.at[a, slot, 0:rows],
            send_sem=ag_send.at[a, slot, 0 if to is above else 1],
            recv_sem=ag_recv.at[a, slot],
            device_id=to,
            device_id_type=MESH,
        )

    def pair_copy(a, slot):
        return pltpu.make_async_remote_copy(
            src_ref=rows_in.at[a, slot, 0:rows],
            dst_ref=rows_in.at[a, slot, rows : 2 * rows],
            send_sem=pair_send.at[a, slot],
            recv_sem=pair_recv.at[a, slot],
            device_id=partner,
            device_id_type=MESH,
        )

    def op_copy(a, slot):
        return pltpu.make_async_remote_copy(
            src_ref=out.at[a, slot, rows : 2 * rows],
            dst_ref=pair_in.at[a, slot],
            send_sem=op_send.at[a, slot],
            recv_sem=op_recv.at[a, slot],
            device_id=partner,
            device_id_type=MESH,
        )

    def rs_copy(a, slot, arrive, to):
        return pltpu.make_async_remote_copy(
            src_ref=out.at[a, slot, 0:rows],
            dst_ref=line_in.at[a, arrive],
            send_sem=rs_send.at[a, slot],
            recv_sem=rs_recv.at[a, arrive],
            device_id=to,
            device_id_type=MESH,
        )

    def half_of(i, which):
        count = sources[i].shape[1] // 2
        return pl.ds(pl.multiple_of(which * count, count), count)

    def x_copy(i):
        return pltpu.make_async_remote_copy(
            src_ref=sources[i].at[0, half_of(i, group)],
            dst_ref=weight_ref(i, 1, half_of(i, group)),
            send_sem=x_send.at[i],
            recv_sem=x_recv.at[i],
            device_id=x_mate,
            device_id_type=MESH,
        )

    def y_copy(i):
        return pltpu.make_async_remote_copy(
            src_ref=weight_ref(i, 1, half_of(i, group)),
            dst_ref=weight_ref(i, 1, half_of(i, group)),
            send_sem=y_send.at[i],
            recv_sem=y_recv.at[i],
            device_id=y_mate,
            device_id_type=MESH,
        )

    def w_copy(d, p):
        there = (z + d) % planes
        return pltpu.make_async_remote_copy(
            src_ref=w_send.at[2 * there + (core if p == 0 else 1 - core)],
            dst_ref=w_in.at[2 * z + p],
            send_sem=w_sems.at[0],
            recv_sem=w_sems.at[1],
            device_id=at(there, p),
            device_id_type=MESH,
        )

    def g_copy(d, p):
        there = (z + d) % planes
        return pltpu.make_async_remote_copy(
            src_ref=g_send.at[2 * there + p],
            dst_ref=g_in.at[2 * z + core],
            send_sem=g_sems.at[0],
            recv_sem=g_sems.at[1],
            device_id=at(there, p),
            device_id_type=MESH,
        )

    def send_on(a, slot, upward):
        if upward:
            @pl.when(z < planes - 1)
            def _():
                ag_copy(a, slot, above).start()
        else:
            @pl.when(z > 0)
            def _():
                ag_copy(a, slot, below).start()

    for a in range(2):
        send_on(a, z, True)
        send_on(a, z, False)
    for i in range(3):
        x_copy(i).start()
    for a in range(2):
        pair_copy(a, z).start()

    shape = (8 * n, rows)
    place_of = lax.broadcasted_iota(jnp.int32, shape, 0) // 8
    expert_of = (place_of // 4 * 2 + place_of % 2) * 2 + place_of // 2 % 2
    by_expert = jnp.zeros(shape, F32)
    for k in range(top):
        by_expert = by_expert + jnp.where(ids_ref[k : k + 1, :] == expert_of, rw_ref[k : k + 1, :], 0.0)
    w_send[...] = by_expert.reshape(n // 2, 2, 8, rows)
    for d, p in line:
        w_copy(d, p).start()
    w_in[2 * z] = w_send[2 * z + core]

    for load in loads[2:]:
        load.wait()
    for a in range(2):
        pair_copy(a, z).wait_recv()
    every = w_in.at[1 : 2 * planes]
    pltpu.make_async_copy(every, every, w_sems.at[1]).wait()
    w_col[...] = w_in[...].reshape(8 * n, rows).T

    def column(slot, p, whose):
        lane = lax.broadcasted_iota(jnp.int32, (rows, 8 * n), 1)
        wanted = ((2 * slot + p) * 2 + whose) * 8
        return jnp.sum(jnp.where(lane == wanted, w_col[...], 0.0), axis=1, keepdims=True)

    def compute(e, slot):
        whose = side if e == 0 else 1 - side
        x = rows_in[0, slot]
        g = rows_in[1, slot]
        weight = jnp.concatenate([column(slot, 0, whose), column(slot, 1, whose)], axis=0)
        both = jnp.dot(x, both_ref[e], preferred_element_type=F32)
        gate_pre, up_value = both[:, 0:wide], both[:, wide : 2 * wide]
        hidden_grad = lax.dot_general(g, down_ref[e], NT, preferred_element_type=F32)
        sig = 0.5 * jnp.tanh(0.5 * gate_pre) + 0.5
        act = gate_pre * sig
        hidden = act * up_value
        inner = (hidden * hidden_grad).astype(BF16)
        ones = jnp.ones((8, inner.shape[1]), BF16)
        inner_rows = lax.dot_general(ones, inner, NT, preferred_element_type=F32)
        g_send[2 * slot, whose] = inner_rows[:, 0:rows]
        g_send[2 * slot + 1, whose] = inner_rows[:, rows : 2 * rows]
        mix = jnp.dot((hidden * weight).astype(BF16), down_ref[e], preferred_element_type=F32)
        scaled = hidden_grad * weight
        gate_grad = (scaled * up_value * (sig * (1.0 + gate_pre * (1.0 - sig)))).astype(BF16)
        up_grad = (scaled * act).astype(BF16)
        grads = jnp.concatenate([gate_grad, up_grad], axis=1)
        slot_grad = lax.dot_general(grads, both_ref[e], NT, preferred_element_type=F32)
        if e == 0:
            acc[0, slot] = mix
            acc[1, slot] = slot_grad
        else:
            out[0, slot] = (acc[0, slot] + mix).astype(BF16)
            out[1, slot] = (acc[1, slot] + slot_grad).astype(BF16)
            for a in range(2):
                op_copy(a, slot).start()

    def arrivals(s):
        for a in range(2):
            @pl.when(z - s >= 0)
            def _():
                ag_copy(a, z - s, above).wait_recv()
                send_on(a, z - s, True)
                pair_copy(a, z - s).start()

            @pl.when(z + s < planes)
            def _():
                ag_copy(a, z + s, below).wait_recv()
                send_on(a, z + s, False)
                pair_copy(a, z + s).start()

    def first_pass(s):
        @pl.loop(0, 2)
        def _(j):
            slot = z - s + 2 * s * j

            @pl.when((slot >= 0) & (slot < planes))
            def _():
                for a in range(2):
                    pair_copy(a, slot).wait_recv()
                compute(0, slot)

    def pass_on(i):
        x_copy(i).wait_recv()
        y_copy(i).start()

    def line_step(dest, upward, wanted):
        first = 0 if upward else planes - 1

        def send(a):
            if upward:
                @pl.when(z + 1 == dest)
                def _():
                    rs_copy(a, dest, planes, above).start()

                @pl.when(z + 1 != dest)
                def _():
                    rs_copy(a, dest, dest, above).start()
            else:
                rs_copy(a, dest, dest, below).start()

        def add(a, arrived):
            op_copy(a, dest).wait_recv()
            total = out[a, dest, 0:rows].astype(F32) + pair_in[a, dest].astype(F32)
            if arrived:
                rs_copy(a, dest, dest, above).wait_recv()
                total = total + line_in[a, dest].astype(F32)
            out[a, dest, 0:rows] = total.astype(BF16)
            send(a)

        @pl.when(wanted & (z < dest if upward else z > dest))
        def _():
            @pl.when(z != first)
            def _():
                for a in range(2):
                    add(a, True)

            @pl.when(z == first)
            def _():
                for a in range(2):
                    add(a, False)

    upward = [planes - 2, planes - 1] + list(range(planes - 3, 0, -1))
    table = []
    for zz in range(planes):
        low = zz < planes // 2
        order = [u if low else planes - 1 - u for u in upward + [0]]
        table.append([u for u in order if u != zz] + [zz])

    def turn(k):
        slot = 0
        for zz in range(planes):
            slot = slot + table[zz][k] * (z == zz).astype(jnp.int32)
        return slot

    compute(0, z)
    last = planes - 1
    for s in range(1, last):
        arrivals(s)
        if s <= 2:
            pass_on(s - 1)
        first_pass(s)
    pass_on(2)
    for i in range(3):
        y_copy(i).wait_recv()
    inner = (z > 0) & (z < last)
    high = z >= planes // 2

    def second_pass(begin, end, wanted):
        @pl.when(wanted)
        def _():
            @pl.loop(begin, end)
            def _(j):
                slot = 0
                for jj in range(begin, end):
                    slot = slot + turn(jj) * (j == jj).astype(jnp.int32)
                compute(1, slot)

    compute(1, turn(0))
    second_pass(1, 4, inner)
    for k, u in enumerate(upward):
        line_step(planes - 1 - u, False, high)
        line_step(u, True, z >= 0)
        line_step(planes - 1 - u, False, z < planes // 2)
        if k == 0:
            arrivals(last)
            first_pass(last)
            second_pass(1, 3, (z == 0) | (z == last))
        elif k == 1:
            second_pass(3, 4, (z == 0) | (z == last))
        elif k + 2 < planes:
            compute(1, turn(k + 2))
    for d, p in line:
        g_copy(d, p).start()
    g_in[2 * z + core] = g_send[2 * z]

    every = g_in.at[1 : 2 * planes]
    pltpu.make_async_copy(every, every, g_sems.at[1]).wait()
    ids = ids_ref[...]
    picked = jnp.zeros((top, rows), F32)
    for e in range(n):
        picked = jnp.where(ids == e, g_in[e // 4 * 2 + e % 2, e // 2 % 2][0:top], picked)
    wgrad_ref[...] = picked

    for a in range(2):
        op_copy(a, z).wait_recv()
        total = out[a, z, 0:rows].astype(F32) + pair_in[a, z].astype(F32)
        acc[a, z, 0:rows] = total

        @pl.when(z > 0)
        def _():
            rs_copy(a, z, planes, above).wait_recv()
            acc[a, z, 0:rows] = acc[a, z, 0:rows] + line_in[a, planes].astype(F32)

        @pl.when(z < planes - 1)
        def _():
            rs_copy(a, z, z, below).wait_recv()
            acc[a, z, 0:rows] = acc[a, z, 0:rows] + line_in[a, z].astype(F32)

    mixed_ref[...] = acc[0, z, 0:rows].astype(BF16)
    tgrad_ref[...] = acc[1, z, 0:rows].astype(BF16)

    for a in range(2):
        for slot in range(planes):
            @pl.when((slot <= z) & (z < planes - 1))
            def _():
                ag_copy(a, slot, above).wait_send()

            @pl.when((slot >= z) & (z > 0))
            def _():
                ag_copy(a, slot, below).wait_send()

            @pl.when(slot != z)
            def _():
                rs_copy(a, slot, slot, above).wait_send()

            pair_copy(a, slot).wait_send()
            op_copy(a, slot).wait_send()
    for i in range(3):
        x_copy(i).wait_send()
        y_copy(i).wait_send()
    every = w_send.at[1 : 2 * planes]
    pltpu.make_async_copy(every, every, w_sems.at[0]).wait()
    every = g_send.at[1 : 2 * planes]
    pltpu.make_async_copy(every, every, g_sems.at[0]).wait()


def line_device(tokens, cotangent, expert_ids, router_weights, seq_lengths, w_gate, w_up, w_down):
    n = lax.axis_size("ctx")
    planes = n // 4
    rows, depth = tokens.shape
    hidden = w_gate.shape[2]
    top = expert_ids.shape[1]
    vmem = pl.BlockSpec(memory_space=pltpu.VMEM)
    hbm = pl.BlockSpec(memory_space=pl.ANY)
    dma = pltpu.SemaphoreType.DMA
    mixed, token_grads, weight_grads = pl.pallas_call(
        functools.partial(line_kernel, n, rows * 4.0),
        out_shape=(
            jax.ShapeDtypeStruct(tokens.shape, BF16),
            jax.ShapeDtypeStruct(tokens.shape, BF16),
            jax.ShapeDtypeStruct((top, rows), F32),
        ),
        in_specs=[pl.BlockSpec(memory_space=pltpu.SMEM)] + [hbm] * 2 + [vmem] * 2 + [hbm] * 3,
        out_specs=(vmem, vmem, vmem),
        scratch_shapes=[
            pltpu.VMEM((2, depth, 2 * hidden), BF16),
            pltpu.VMEM((2, hidden, depth), BF16),
            pltpu.VMEM((rows, depth), BF16),
            pltpu.VMEM((2, planes, 2 * rows, depth), BF16),
            pltpu.VMEM((2, planes, 2 * rows, depth), F32),
            pltpu.VMEM((2, planes, 2 * rows, depth), BF16),
            pltpu.VMEM((2, planes, rows, depth), BF16),
            pltpu.VMEM((2, planes + 1, rows, depth), BF16),
            pltpu.VMEM((n // 2, 2, 8, rows), F32),
            pltpu.VMEM((n // 2, 2, 8, rows), F32),
            pltpu.VMEM((rows, 8 * n), F32),
            pltpu.VMEM((n // 2, 2, 8, rows), F32),
            pltpu.VMEM((n // 2, 2, 8, rows), F32),
            dma((5,)),
            dma((3,)),
            dma((3,)),
            dma((3,)),
            dma((3,)),
            dma((2, planes, 2)),
            dma((2, planes)),
            dma((2, planes)),
            dma((2, planes)),
            dma((2, planes)),
            dma((2, planes)),
            dma((2, planes)),
            dma((2, planes + 1)),
            dma((2,)),
            dma((2,)),
        ],
        compiler_params=pltpu.CompilerParams(
            collective_id=0, has_side_effects=True, vmem_limit_bytes=63 * 1024 * 1024
        ),
        cost_estimate=pl.CostEstimate(
            flops=12 * n * rows * w_gate.size, bytes_accessed=6 * w_gate.size, transcendentals=0
        ),
    )(seq_lengths, tokens, cotangent, expert_ids.T, router_weights.T, w_gate, w_up, w_down)
    return mixed, token_grads, weight_grads.T


def line_fits(mesh, arrays):
    tokens, _, expert_ids, _, _, w_gate = arrays[:6]
    n = mesh.shape["ctx"]
    rows = tokens.shape[0] // (mesh.shape["groups"] * n * mesh.shape["dp"])
    held = 2 * n * rows * tokens.shape[1] * 9
    return (
        mesh.shape["dp"] == 1
        and mesh.shape["groups"] == 2
        and w_gate.shape[0] == n
        and w_gate.shape[1] % 32 == 0
        and w_gate.shape[2] % 32 == 0
        and n % 8 == 0
        and n >= 16
        and expert_ids.shape[1] <= 8
        and rows % 128 == 0
        and held <= 40 * 1024 * 1024
    )


def loss_scale(position, seq_lengths, mean_length):
    ends = jnp.cumsum(seq_lengths)
    starts = ends - seq_lengths
    inside = (position[:, None] >= starts[None, :]) & (position[:, None] < ends[None, :])
    own_length = jnp.sum(jnp.where(inside, seq_lengths[None, :], 0), axis=1)
    return mean_length / own_length.astype(jnp.float32)


def forward_rows(slot_rows, gate_full, up_full, down_full):
    gate_pre = jnp.dot(slot_rows, gate_full, preferred_element_type=jnp.float32)
    up_value = jnp.dot(slot_rows, up_full, preferred_element_type=jnp.float32)
    activated = jax.nn.silu(gate_pre)
    hidden = (activated * up_value).astype(jnp.bfloat16)
    expert_out = jnp.dot(hidden, down_full, preferred_element_type=jnp.float32).astype(jnp.bfloat16)
    return (gate_pre, up_value, activated, expert_out)


def backward_rows(grad_rows, gate_pre, up_value, activated, gate_full, up_full, down_full):
    contract = (((1,), (1,)), ((), ()))
    hidden_grad = lax.dot_general(
        grad_rows, down_full, contract, preferred_element_type=jnp.float32
    )
    sigmoid_value = jax.nn.sigmoid(gate_pre)
    silu_slope = sigmoid_value * (1.0 + gate_pre * (1.0 - sigmoid_value))
    gate_grad = (hidden_grad * up_value * silu_slope).astype(jnp.bfloat16)
    up_grad = (hidden_grad * activated).astype(jnp.bfloat16)
    slot_grad = lax.dot_general(gate_grad, gate_full, contract, preferred_element_type=jnp.float32)
    slot_grad = slot_grad + lax.dot_general(
        up_grad, up_full, contract, preferred_element_type=jnp.float32
    )
    return slot_grad.astype(jnp.bfloat16)


def slot_ranks(flat_ids, experts):
    expert_hits = (flat_ids[:, None] == jnp.arange(experts, dtype=jnp.int32)[None, :]).astype(
        jnp.int32
    )
    assign_count = flat_ids.shape[0]
    row_iota = lax.broadcasted_iota(jnp.int32, (assign_count, assign_count), 0)
    col_iota = lax.broadcasted_iota(jnp.int32, (assign_count, assign_count), 1)
    lower_mask = (row_iota > col_iota).astype(jnp.bfloat16)
    earlier = jnp.dot(
        lower_mask, expert_hits.astype(jnp.bfloat16), preferred_element_type=jnp.float32
    )
    return jnp.sum(earlier * expert_hits.astype(jnp.float32), axis=1).astype(jnp.int32)


def per_device(tokens, cotangent, expert_ids, router_weights, seq_lengths, w_gate, w_up, w_down):
    ctx_count = lax.axis_size("ctx")
    dp_count = lax.axis_size("dp")
    row_count, top_count = expert_ids.shape
    slot_cap = max(2, min(row_count, row_count * top_count * 5 // (4 * ctx_count)))
    block_index = lax.axis_index("ctx") * dp_count + lax.axis_index("dp")
    position = block_index * row_count + jnp.arange(row_count, dtype=jnp.int32)
    loss_weight = loss_scale(position, seq_lengths, row_count * 4.0)
    out_grad = (cotangent.astype(jnp.float32) * loss_weight[:, None]).astype(jnp.bfloat16)
    flat_ids = expert_ids.reshape(-1)
    assign_count = flat_ids.shape[0]
    dest_slot = flat_ids * slot_cap + slot_ranks(flat_ids, ctx_count)
    source_row = jnp.full((ctx_count * slot_cap,), assign_count, jnp.int32)
    source_row = source_row.at[dest_slot].set(jnp.arange(assign_count, dtype=jnp.int32))
    filled = source_row < assign_count
    token_of = jnp.minimum(source_row, assign_count - 1) // top_count
    zero_value = jnp.zeros((), jnp.bfloat16)
    token_send = jnp.where(filled[:, None], tokens[token_of], zero_value).reshape(
        ctx_count, slot_cap, -1
    )
    grad_send = jnp.where(filled[:, None], out_grad[token_of], zero_value).reshape(
        ctx_count, slot_cap, -1
    )
    gate_full, up_full, down_full = (
        lax.all_gather(w_gate[0], "dp", axis=0, tiled=True),
        lax.all_gather(w_up[0], "dp", axis=0, tiled=True),
        lax.all_gather(w_down[0], "dp", axis=1, tiled=True),
    )
    token_arrived = lax.all_to_all(token_send, "ctx", split_axis=0, concat_axis=0, tiled=True)
    grad_arrived = lax.all_to_all(grad_send, "ctx", split_axis=0, concat_axis=0, tiled=True)
    source_count = token_arrived.shape[0]
    slot_count = token_arrived.shape[1]
    slot_rows = token_arrived.reshape(source_count * slot_count, -1)
    grad_rows = grad_arrived.reshape(source_count * slot_count, -1)
    gate_pre, up_value, activated, expert_out = forward_rows(
        slot_rows, gate_full, up_full, down_full
    )
    out_blocks = expert_out.reshape(source_count, slot_count, -1)
    slot_grad = backward_rows(
        grad_rows, gate_pre, up_value, activated, gate_full, up_full, down_full
    )
    out_home = lax.all_to_all(out_blocks, "ctx", split_axis=0, concat_axis=0, tiled=True)
    grad_home = lax.all_to_all(
        slot_grad.reshape(source_count, slot_count, -1),
        "ctx",
        split_axis=0,
        concat_axis=0,
        tiled=True,
    )
    out_rows = out_home.reshape(ctx_count * slot_cap, -1)[dest_slot].reshape(
        row_count, top_count, -1
    )
    grad_rows = grad_home.reshape(ctx_count * slot_cap, -1)[dest_slot].reshape(
        row_count, top_count, -1
    )
    mixed = jnp.sum(router_weights[:, :, None] * out_rows.astype(jnp.float32), axis=1).astype(
        jnp.bfloat16
    )
    token_grads = jnp.sum(
        router_weights[:, :, None] * grad_rows.astype(jnp.float32), axis=1
    ).astype(jnp.bfloat16)
    weight_grads = jnp.einsum("td,tkd->tk", out_grad, out_rows, preferred_element_type=jnp.float32)
    return (mixed, token_grads, weight_grads)


def solution(mesh):
    in_specs = (
        P(("groups", "ctx", "dp"), None),
        P(("groups", "ctx", "dp"), None),
        P(("groups", "ctx", "dp"), None),
        P(("groups", "ctx", "dp"), None),
        P("groups"),
        P("ctx", "dp", None),
        P("ctx", "dp", None),
        P("ctx", None, "dp"),
    )
    out_specs = (
        P(("groups", "ctx", "dp"), None),
        P(("groups", "ctx", "dp"), None),
        P(("groups", "ctx", "dp"), None),
    )

    def run(*arrays):
        plan = line_device if line_fits(mesh, arrays) else per_device
        return jax.shard_map(
            plan, mesh=mesh, in_specs=in_specs, out_specs=out_specs, check_vma=False
        )(*arrays)

    return run
```
